32 devices in a mesh: segment: 2 (over core), expert: 16 (over z, y, x).
Axes of the slice: x: 2, y: 2, z: 4, core: 2. Of those that a mesh axis runs over, the one named last changes fastest.
Arguments:
- inputs: bfloat16 [2, 1024, 2560], P(None, 'expert'), may hold values from -6 to 6
- cotangent: bfloat16 [2, 1024, 2560], P(None, 'expert'), may hold values from -6 to 6
- norm_gain: float32 [2, 2560], P('segment'), may hold values from 0.5 to 1.5
- routes: int32 [2, 2, 1024, 6], P('segment', None, 'expert'), may hold values from 0 to 15, all different within a row; in each aligned block of 64 rows (0 to 63, 64 to 127, ..., all dimensions but the last counted through in order) at most 32 rows name the same one
- route_gates: float32 [2, 2, 1024, 6], P('segment', None, 'expert'), may hold values from 0.05 to 1
- w_gate: bfloat16 [2, 16, 2560, 768], P('segment', 'expert'), may hold values from -0.125 to 0.125
- w_up: bfloat16 [2, 16, 2560, 768], P('segment', 'expert'), may hold values from -0.125 to 0.125
- w_down: bfloat16 [2, 16, 768, 2560], P('segment', 'expert'), may hold values from -0.21875 to 0.21875
Outputs:
- states: bfloat16 [2, 2, 1024, 2560], P('segment', None, 'expert')
- input_grads: bfloat16 [2, 2, 1024, 2560], P('segment', None, 'expert')
The draws below stay inside these ranges and needn't reach their ends.
Inputs may be any that keep to these rules, and one draw needn't show every extreme that they name: `routes`: within the 64 tokens of one device in one micro-batch and layer, no expert is named by more than 32 tokens, a bound that some block reaches; each token names 6 different experts.
All inputs are finite; a program needn't handle non-finite values.
Results may differ from the reference program's by a relative error of at most 0.024.
Values may be sent and summed in bfloat16 or wider, within the bound.
A program may use at most 192 MiB of HBM per device.

```python
import math
import jax
import jax.numpy as jnp
import numpy as np
from jax import lax

D = 2560
H = 768
TOP = 6
MICRO = 2
TOK_MB = 64
LAYERS = 2
EXPERTS = 16
TOKENS = 1024
CAP = 32
N_EXPERT = 16


def steps_of(rng, dims, split, least, high):
    def one(axis_at, parts):
        steps = jax.random.uniform(jax.random.fold_in(jax.random.fold_in(rng, 6), axis_at), (parts,), jnp.float32, least / len(split), high / len(split))
        return jnp.repeat(jnp.exp(steps), dims[axis_at] // parts).reshape((-1,) + (1,) * (len(dims) - axis_at - 1))

    gain = one(*split[0])
    for cut in split[1:]:
        gain = gain * one(*cut)
    return gain


def routed_block(rng, own, number, rows, amount, top, most, slope):
    order = jax.random.permutation(rng, amount)
    packed, common = portions_of(amount, rows * top, most, slope, True), portions_of(amount, rows * top, most, slope, False)
    places = jnp.arange(amount)

    def named(lengths, turn):
        used = int((lengths > 0).sum())
        fixed = max(1, used // 4)
        shifted = fixed + (places - fixed + turn * (used - fixed)) % max(1, amount - fixed)
        return jnp.zeros((amount,), jnp.int32).at[order[jnp.where(places < fixed, places, shifted)]].set(jnp.asarray(lengths, jnp.int32))

    lengths = jnp.where(number % 4 == 0, named(packed, number // 4), named(common, number - number // 4 - 1))
    mixed = jax.random.permutation(jax.random.fold_in(own, 3), amount)
    source_of, receiver = mixed[0:amount // 2 * 2:2], mixed[1:amount // 2 * 2:2]
    margin = jnp.minimum(lengths[source_of] - 1, most - lengths[receiver]) // 2
    margin = jnp.where((source_of == order[0]) | (receiver == order[0]) | (lengths[receiver] == 0), 0, jnp.maximum(margin, 0))
    shifted = jax.random.randint(jax.random.fold_in(own, 4), (amount // 2,), 0, 1 << 20) % (margin + 1)
    lengths = lengths.at[source_of].add(-shifted).at[receiver].add(shifted)
    labels = jnp.searchsorted(jnp.cumsum(lengths), jnp.arange(rows * top), side="right").astype(jnp.int32)
    listing = labels.reshape(top, rows).T
    listing = listing[jax.random.permutation(jax.random.fold_in(own, 1), rows)]
    turn = jax.random.randint(jax.random.fold_in(own, 2), (rows, 1), 0, top)
    return jnp.take_along_axis(listing, (jnp.arange(top)[None, :] + turn) % top, axis=1)


def portions_of(number_of, total, bound, lean, full):
    loads = [(1 << 20) // math.isqrt(rank ** lean) + 1 for rank in range(1, number_of + 1)]
    largest = bound if full else min(bound, max(-(-total // number_of), total * loads[0] // sum(loads)))
    least = 1 if total - largest >= number_of - 1 else 0
    holding, rest = [largest] + [least] * (number_of - 1), total - largest - least * (number_of - 1)
    while rest > 0:
        movable = [i for i in range(1, number_of) if holding[i] < largest] or [i for i in range(1, number_of) if holding[i] < bound]
        mass, budget = sum([loads[i] for i in movable]), rest
        for i in movable:
            more = min(bound - holding[i], max(1, budget * loads[i] // mass), rest)
            holding[i] = holding[i] + more
            rest = rest - more
    return np.array(holding)


def noise(stream_key, dims, width, most, cuts=(), kind=jnp.bfloat16):
    values = width * jax.random.normal(stream_key, dims, jnp.float32)
    if cuts:
        values = values * steps_of(stream_key, dims, cuts, -0.22, 0.18)
    return jnp.clip(values, -most, most).astype(kind)


def setup_inputs(seed: int = 0) -> dict:
    key_list = jax.random.split(jax.random.key(seed), 9)
    inputs = noise(key_list[0], (MICRO, TOKENS, D), 1.0, 6.0, ((1, 16),))
    cotangent = noise(key_list[1], (MICRO, TOKENS, D), 1.0, 6.0, ((1, 16),))
    norm_gain = jnp.clip(1.0 + 0.1 * jax.random.normal(key_list[2], (LAYERS, D), jnp.float32), 0.5, 1.5)
    routes_keys = jax.random.split(jax.random.fold_in(key_list[3], 1), LAYERS * MICRO * TOKENS // TOK_MB)
    routes_turns = jax.random.permutation(jax.random.fold_in(key_list[3], 3), LAYERS * MICRO * TOKENS // TOK_MB)
    routes = jax.vmap(lambda own, number: routed_block(jax.random.fold_in(key_list[3], 2), own, number, TOK_MB, EXPERTS, TOP, CAP, 2))(routes_keys, routes_turns).reshape((LAYERS, MICRO, TOKENS, TOP))
    route_gates = jnp.clip(jnp.exp(math.log(1.0) - 2.9957323 * jax.random.uniform(key_list[4], (LAYERS, MICRO, TOKENS, TOP), jnp.float32) ** steps_of(key_list[4], (LAYERS, MICRO, TOKENS, TOP), ((0, 2), (2, 16)), -0.2, 0.2)), 0.05, 1.0)
    w_gate = noise(key_list[5], (LAYERS, EXPERTS, D, H), D ** -0.5, 0.125, ((0, 2), (1, 16)))
    w_up = noise(key_list[6], (LAYERS, EXPERTS, D, H), D ** -0.5, 0.125, ((0, 2), (1, 16)))
    w_down = noise(key_list[7], (LAYERS, EXPERTS, H, D), H ** -0.5, 0.21875, ((0, 2), (1, 16)))
    return dict(inputs=inputs, cotangent=cotangent, norm_gain=norm_gain, routes=routes, route_gates=route_gates, w_gate=w_gate, w_up=w_up, w_down=w_down)


epsilon = 1e-06

def slot_table(route_block, experts, capacity):
    flat_ids = route_block.reshape(-1).astype(jnp.int32)
    onehot = (flat_ids[:, None] == jnp.arange(experts, dtype=jnp.int32)[None, :]).astype(jnp.int32)
    before = jnp.cumsum(onehot, axis=0) - onehot
    position = lax.optimization_barrier(jnp.sum(before * onehot, axis=1)).astype(jnp.int32)
    return (flat_ids * capacity + position).astype(jnp.int32).reshape(route_block.shape)

def expert_forward(row_block, gate_mat, up_mat, down_mat):
    gate_pre = jnp.dot(row_block, gate_mat, preferred_element_type=jnp.float32)
    up_val = jnp.dot(row_block, up_mat, preferred_element_type=jnp.float32)
    activated = (jax.nn.silu(gate_pre) * up_val).astype(jnp.bfloat16)
    expert_out = jnp.dot(activated, down_mat, preferred_element_type=jnp.float32).astype(jnp.bfloat16)
    return (expert_out, gate_pre, up_val)

def expert_backward(d_out, gate_pre, up_val, gate_mat, up_mat, down_mat):
    contract = (((1,), (1,)), ((), ()))
    d_act = lax.dot_general(d_out, down_mat, contract, preferred_element_type=jnp.float32)
    sigmoid_g = jax.nn.sigmoid(gate_pre)
    d_gate = (d_act * up_val * sigmoid_g * (1.0 + gate_pre * (1.0 - sigmoid_g))).astype(jnp.bfloat16)
    d_up = (d_act * gate_pre * sigmoid_g).astype(jnp.bfloat16)
    summed = lax.dot_general(d_gate, gate_mat, contract, preferred_element_type=jnp.float32)
    summed = summed + lax.dot_general(d_up, up_mat, contract, preferred_element_type=jnp.float32)
    return summed.astype(jnp.bfloat16)

def global_slots(route_layer):
    blocks = route_layer.reshape(N_EXPERT, TOK_MB, TOP)
    return jax.vmap(lambda block_ids: slot_table(block_ids, EXPERTS, CAP))(blocks)

def source_ids(slot_ids):
    return jnp.broadcast_to(jnp.arange(N_EXPERT, dtype=jnp.int32)[:, None, None], slot_ids.shape)

def to_experts(spread_rows, slot_ids):
    buffer = jnp.zeros((N_EXPERT, EXPERTS * CAP, D), jnp.bfloat16)
    buffer = buffer.at[source_ids(slot_ids), slot_ids].set(spread_rows)
    buffer = buffer.reshape(N_EXPERT, EXPERTS, CAP, D).transpose(1, 0, 2, 3)
    return buffer.reshape(EXPERTS, N_EXPERT * CAP, D)

def from_experts(expert_rows, slot_ids):
    back_rows = expert_rows.reshape(EXPERTS, N_EXPERT, CAP, D).transpose(1, 0, 2, 3)
    back_rows = back_rows.reshape(N_EXPERT, EXPERTS * CAP, D)
    return back_rows[source_ids(slot_ids), slot_ids]

def forward_layer(layer_in, route_layer, gate_layer, gain_row, gate_mats, up_mats, down_mats):
    wide_in = layer_in.astype(jnp.float32)
    inv_rms = lax.rsqrt(lax.optimization_barrier(jnp.mean(wide_in * wide_in, axis=1, keepdims=True)) + epsilon)
    normed = (wide_in * inv_rms * gain_row).astype(jnp.bfloat16)
    slot_ids = global_slots(route_layer)
    spread = jnp.broadcast_to(normed.reshape(N_EXPERT, TOK_MB, 1, D), (N_EXPERT, TOK_MB, TOP, D))
    rows_all = to_experts(spread, slot_ids)

    def one_expert(pieces):
        return expert_forward(pieces[0], pieces[1], pieces[2], pieces[3])
    expert_out, gate_pre, up_val = lax.map(one_expert, (rows_all, gate_mats, up_mats, down_mats))
    picked = from_experts(expert_out, slot_ids).reshape(TOKENS, TOP, D)
    mixed_sum = lax.optimization_barrier(jnp.sum(gate_layer[:, :, None] * picked.astype(jnp.float32), axis=1))
    return ((wide_in + mixed_sum).astype(jnp.bfloat16), gate_pre, up_val)

def backward_layer(d_in, layer_in, route_layer, gate_layer, gain_row, gate_pre, up_val, gate_mats, up_mats, down_mats):
    wide_in = layer_in.astype(jnp.float32)
    inv_rms = lax.rsqrt(lax.optimization_barrier(jnp.mean(wide_in * wide_in, axis=1, keepdims=True)) + epsilon)
    d_wide = d_in.astype(jnp.float32)
    slot_ids = global_slots(route_layer)
    d_out = (gate_layer[:, :, None] * d_wide[:, None, :]).astype(jnp.bfloat16)
    rows_all = to_experts(d_out.reshape(N_EXPERT, TOK_MB, TOP, D), slot_ids)

    def one_expert(pieces):
        return expert_backward(pieces[0], pieces[1], pieces[2], pieces[3], pieces[4], pieces[5])
    d_rows = lax.map(one_expert, (rows_all, gate_pre, up_val, gate_mats, up_mats, down_mats))
    picked = from_experts(d_rows, slot_ids).reshape(TOKENS, TOP, D)
    d_norm = lax.optimization_barrier(jnp.sum(picked.astype(jnp.float32), axis=1))
    scaled = gain_row * d_norm
    inner = lax.optimization_barrier(jnp.mean(wide_in * scaled, axis=1, keepdims=True))
    cubed = inv_rms * inv_rms * inv_rms
    return (d_wide + inv_rms * scaled - wide_in * cubed * inner).astype(jnp.bfloat16)

def reference(inputs, cotangent, norm_gain, routes, route_gates, w_gate, w_up, w_down):
    state_list = []
    grad_list = []
    for micro_no in range(MICRO):
        layer_in = inputs[micro_no]
        kept_vals = []
        outs_here = []
        for layer_no in range(LAYERS):
            layer_out, gate_pre, up_val = forward_layer(layer_in, routes[layer_no, micro_no], route_gates[layer_no, micro_no], norm_gain[layer_no], w_gate[layer_no], w_up[layer_no], w_down[layer_no])
            kept_vals.append((layer_in, gate_pre, up_val))
            outs_here.append(layer_out)
            layer_in = layer_out
        d_in = cotangent[micro_no]
        grads_here = [None] * LAYERS
        for layer_no in reversed(range(LAYERS)):
            saved_in, gate_pre, up_val = kept_vals[layer_no]
            d_in = backward_layer(d_in, saved_in, routes[layer_no, micro_no], route_gates[layer_no, micro_no], norm_gain[layer_no], gate_pre, up_val, w_gate[layer_no], w_up[layer_no], w_down[layer_no])
            grads_here[layer_no] = d_in
        state_list.append(jnp.stack(outs_here))
        grad_list.append(jnp.stack(grads_here))
    return (jnp.stack(state_list, axis=1), jnp.stack(grad_list, axis=1))
```

```python
import jax
import jax.numpy as jnp
from jax import lax
from jax.sharding import PartitionSpec as P

EPS = 1e-06
F32 = jnp.float32
BF = jnp.bfloat16
CONTRACT = (((1,), (1,)), ((), ()))


def passed_along(shard, by):
    peers = lax.axis_size("segment")
    pairs = [(i, i + by) for i in range(peers) if 0 <= i + by < peers]
    return lax.ppermute(shard, "segment", pairs)


def inverse_rms(wide):
    return lax.rsqrt(jnp.mean(wide * wide, axis=1, keepdims=True) + EPS)


def pick(items, index):
    return lax.dynamic_index_in_dim(items, index, 0, keepdims=False)


def gather_rows(rows):
    return lax.all_gather(rows, "expert", axis=0, tiled=True)


def scatter_sum(rows):
    return lax.psum_scatter(rows, "expert", scatter_dimension=0, tiled=True)


def forward_stage(layer_in, gate_col, gain_row, gate_mat, up_mat, down_mat):
    wide = layer_in.astype(F32)
    normed = (wide * inverse_rms(wide) * gain_row).astype(BF)
    rows = gather_rows(normed)
    gate_pre = jnp.dot(rows, gate_mat, preferred_element_type=F32)
    up_val = jnp.dot(rows, up_mat, preferred_element_type=F32)
    activated = (jax.nn.silu(gate_pre) * up_val).astype(BF)
    out = jnp.dot(activated, down_mat, preferred_element_type=F32)
    mixed = scatter_sum((out * gate_col[:, None]).astype(BF))
    return (wide + mixed.astype(F32)).astype(BF), gate_pre, up_val


def backward_stage(d_in, layer_in, gate_col, gain_row, gate_pre, up_val, gate_mat, up_mat, down_mat):
    rows = gather_rows(d_in)
    d_out = (gate_col[:, None] * rows.astype(F32)).astype(BF)
    d_act = lax.dot_general(d_out, down_mat, CONTRACT, preferred_element_type=F32)
    sig = jax.nn.sigmoid(gate_pre)
    d_gate = (d_act * up_val * sig * (1.0 + gate_pre * (1.0 - sig))).astype(BF)
    d_up = (d_act * gate_pre * sig).astype(BF)
    summed = lax.dot_general(d_gate, gate_mat, CONTRACT, preferred_element_type=F32)
    summed = summed + lax.dot_general(d_up, up_mat, CONTRACT, preferred_element_type=F32)
    d_norm = scatter_sum(summed.astype(BF)).astype(F32)
    wide = layer_in.astype(F32)
    inv = inverse_rms(wide)
    scaled = gain_row * d_norm
    inner = jnp.mean(wide * scaled, axis=1, keepdims=True)
    return (d_in.astype(F32) + inv * scaled - wide * (inv * inv * inv) * inner).astype(BF)


def local(inputs, cotangent, norm_gain, routes, route_gates, w_gate, w_up, w_down):
    seg = lax.axis_index("segment")
    segs = lax.axis_size("segment")
    n = lax.axis_size("expert")
    micro, tok, _ = inputs.shape
    mats = (w_gate[0, 0], w_up[0, 0], w_down[0, 0])
    gain_row = norm_gain[0]
    ids = jnp.arange(n, dtype=jnp.int32)
    hit = routes[0][..., None] == ids
    dense = jnp.sum(jnp.where(hit, route_gates[0][..., None], 0.0), axis=2)
    cols = lax.all_to_all(dense.transpose(2, 0, 1), "expert", split_axis=0, concat_axis=0, tiled=True)
    cols = cols.transpose(1, 0, 2).reshape(micro, n * tok)
    ticks = micro + segs - 1
    ins, outs, pres, ups = [], [], [], []
    incoming = jnp.zeros(inputs.shape[1:], BF)
    for t in range(ticks):
        at = jnp.clip(t - seg, 0, micro - 1)
        layer_in = jnp.where(seg == 0, pick(inputs, at), incoming)
        out, pre, up = forward_stage(layer_in, pick(cols, at), gain_row, *mats)
        ins.append(layer_in)
        outs.append(out)
        pres.append(pre)
        ups.append(up)
        if t + 1 < ticks:
            incoming = passed_along(out, 1)
    states = lax.dynamic_slice_in_dim(jnp.stack(outs), seg, micro, 0)
    ins, pres, ups = jnp.stack(ins), jnp.stack(pres), jnp.stack(ups)
    grads = []
    incoming = jnp.zeros(inputs.shape[1:], BF)
    for t in range(ticks):
        at = jnp.clip(t - (segs - 1 - seg), 0, micro - 1)
        d_in = jnp.where(seg == segs - 1, pick(cotangent, at), incoming)
        d_prev = backward_stage(
            d_in, pick(ins, at + seg), pick(cols, at), gain_row, pick(pres, at + seg), pick(ups, at + seg), *mats
        )
        grads.append(d_prev)
        if t + 1 < ticks:
            incoming = passed_along(d_prev, -1)
    grads = lax.dynamic_slice_in_dim(jnp.stack(grads), segs - 1 - seg, micro, 0)
    return states[None], grads[None]


def solution(mesh):
    placed = (
        P(None, "expert", None),
        P(None, "expert", None),
        P("segment", None),
        P("segment", None, "expert", None),
        P("segment", None, "expert", None),
        P("segment", "expert", None, None),
        P("segment", "expert", None, None),
        P("segment", "expert", None, None),
    )
    return jax.shard_map(
        local,
        mesh=mesh,
        in_specs=placed,
        out_specs=(P("segment", None, "expert", None), P("segment", None, "expert", None)),
        check_vma=False,
    )
```

```python
import jax
import jax.numpy as jnp
from jax import lax
from jax.experimental import pallas as pl
from jax.experimental.pallas import tpu as pltpu
from jax.sharding import PartitionSpec as P

EPS = 1e-06
F32 = jnp.float32
BF = jnp.bfloat16
CONTRACT = (((1,), (1,)), ((), ()))


def passed_along(shard, by):
    peers = lax.axis_size("segment")
    pairs = [(i, i + by) for i in range(peers) if 0 <= i + by < peers]
    return lax.ppermute(shard, "segment", pairs)


def inverse_rms(wide):
    return lax.rsqrt(jnp.mean(wide * wide, axis=1, keepdims=True) + EPS)


def pick(items, index):
    return lax.dynamic_index_in_dim(items, index, 0, keepdims=False)


def place():
    n = lax.axis_size("expert")
    me = lax.axis_index("expert")
    deep = n // 4
    high = me // 4
    low = me % 4
    flip_x = low + 1 - 2 * (low % 2)
    flip_y = (low + 2) % 4
    flip_xy = (flip_x + 2) % 4

    def at(step, corner):
        return lax.rem(high + step, deep) * 4 + corner

    return deep, at, low, flip_x, flip_y, flip_xy


def remote(src, dst, sems, at, target):
    return pltpu.make_async_remote_copy(
        src_ref=src,
        dst_ref=dst,
        send_sem=sems[0].at[at],
        recv_sem=sems[1].at[at],
        device_id={"expert": target},
        device_id_type=pl.DeviceIdType.MESH,
    )


def greet():
    deep, at, low, flip_x, flip_y, _ = place()
    barrier = pltpu.get_barrier_semaphore()
    peers = [at(0, flip_x), at(0, flip_y)] + [at(d, low) for d in range(1, deep)]
    for peer in peers:
        pl.semaphore_signal(barrier, inc=1, device_id={"expert": peer}, device_id_type=pl.DeviceIdType.MESH)
    pl.semaphore_wait(barrier, len(peers))


def halves(width):
    cut = width // 256 * 128
    return pl.ds(0, cut), pl.ds(cut, width - cut)


def gather_body(own, out, *sems):
    deep, at, low, flip_x, flip_y, flip_xy = place()
    first, second = halves(own.shape[1])
    greet()
    to_x, to_y = at(0, flip_x), at(0, flip_y)
    started = []

    def send(src, slot, cols, number, target):
        dst = out.at[slot] if cols is None else out.at[slot, :, cols]
        copy = remote(src, dst, sems, number, target)
        copy.start()
        started.append(copy)
        return copy

    along = [None] + [send(own, at(0, low), None, d, at(d, low)) for d in range(1, deep)]
    out[at(0, low)] = own[...]
    relayed = []
    for step in range(deep):
        behind = at(deep - step, low)
        if step:
            along[step].wait_recv()
        base = deep + 6 * step
        block = own if step == 0 else out.at[behind]
        firsts = block.at[:, first]
        seconds = block.at[:, second]
        ax = send(firsts, behind, first, base, to_x)
        by = send(seconds, behind, second, base + 1, to_y)
        bx = send(seconds, behind, second, base + 2, to_x)
        ay = send(firsts, behind, first, base + 3, to_y)
        relayed.append((ax, by, bx, ay))
    last = []
    for step in range(deep):
        base = deep + 6 * step
        ax, by, bx, ay = relayed[step]
        from_x = at(deep - step, flip_x)
        from_y = at(deep - step, flip_y)
        ax.wait_recv()
        last.append(send(out.at[from_x, :, first], from_x, first, base + 4, to_y))
        by.wait_recv()
        last.append(send(out.at[from_y, :, second], from_y, second, base + 5, to_x))
    for _, _, bx, ay in relayed:
        bx.wait_recv()
        ay.wait_recv()
    for copy in last:
        copy.wait_recv()
    for copy in started:
        copy.wait_send()


def scatter_body(parts, out, in_a, in_b, in_x, in_y, in_z, sum_a, sum_b, sum_z, *sems):
    deep, at, low, flip_x, flip_y, flip_xy = place()
    first, second = halves(out.shape[1])
    greet()
    to_x, to_y = at(0, flip_x), at(0, flip_y)
    started = []

    def send(src, dst, number, target):
        copy = remote(src, dst, sems, number, target)
        copy.start()
        started.append(copy)
        return copy

    order = list(range(1, deep)) + [0]
    early, late = {}, {}
    for step in order:
        base = deep + 6 * step
        diag, side_x, side_y = at(step, flip_xy), at(step, flip_x), at(step, flip_y)
        ca = send(parts.at[diag, :, first], in_a.at[step], base, to_y)
        cb = send(parts.at[diag, :, second], in_b.at[step], base + 1, to_x)
        cx = send(parts.at[side_x, :, second], in_x.at[step, :, second], base + 2, to_x)
        cy = send(parts.at[side_y, :, first], in_y.at[step, :, first], base + 3, to_y)
        early[step] = (ca, cb, cx, cy)

    def relay(step):
        base = deep + 6 * step
        side_x, side_y = at(step, flip_x), at(step, flip_y)
        ca, cb, _, _ = early[step]
        ca.wait_recv()
        sum_a[step] = (parts[side_x, :, first].astype(F32) + in_a[step].astype(F32)).astype(BF)
        ex = send(sum_a.at[step], in_x.at[step, :, first], base + 4, to_x)
        cb.wait_recv()
        sum_b[step] = (parts[side_y, :, second].astype(F32) + in_b[step].astype(F32)).astype(BF)
        ey = send(sum_b.at[step], in_y.at[step, :, second], base + 5, to_y)
        late[step] = (ex, ey)

    def joined(step):
        for copy in early[step][2:] + late[step]:
            copy.wait_recv()
        mine = parts[at(step, low)].astype(F32)
        return mine + in_x[step].astype(F32) + in_y[step].astype(F32)

    along = []
    for step in order:
        relay(step)
    for step in order[:-1]:
        sum_z[step] = joined(step).astype(BF)
        along.append(send(sum_z.at[step], in_z.at[step], step, at(step, low)))
    total = joined(0)
    for step, copy in zip(order, along):
        copy.wait_recv()
        total = total + in_z[step].astype(F32)
    out[...] = total
    for copy in started:
        copy.wait_send()


def only_in(span, body):
    def kernel(*refs):
        seg = lax.axis_index("segment")

        @pl.when((seg >= span[0]) & (seg <= span[1]))
        def _():
            body(*refs)

    return kernel


def gather_rows(rows, span, ids):
    n = lax.axis_size("expert")
    tok, width = rows.shape
    copies = n // 4 * 7
    out = pl.pallas_call(
        only_in(span, gather_body),
        out_shape=jax.ShapeDtypeStruct((n, tok, width), rows.dtype),
        in_specs=[pl.BlockSpec(memory_space=pltpu.VMEM)],
        out_specs=pl.BlockSpec(memory_space=pltpu.VMEM),
        scratch_shapes=[pltpu.SemaphoreType.DMA((copies,)), pltpu.SemaphoreType.DMA((copies,))],
        compiler_params=pltpu.CompilerParams(
            collective_id=ids.setdefault(("gather", span), len(ids)),
            has_side_effects=True,
            vmem_limit_bytes=40 << 20,
        ),
        name="gather_rows",
    )(rows)
    return out.reshape(n * tok, width)


def scatter_sum(rows, span, ids):
    n = lax.axis_size("expert")
    width = rows.shape[1]
    tok = rows.shape[0] // n
    deep = n // 4
    copies = deep * 7
    first, second = halves(width)
    return pl.pallas_call(
        only_in(span, scatter_body),
        out_shape=jax.ShapeDtypeStruct((tok, width), F32),
        in_specs=[pl.BlockSpec(memory_space=pltpu.VMEM)],
        out_specs=pl.BlockSpec(memory_space=pltpu.VMEM),
        scratch_shapes=[
            pltpu.VMEM((deep, tok, first.size), BF),
            pltpu.VMEM((deep, tok, second.size), BF),
            pltpu.VMEM((deep, tok, width), BF),
            pltpu.VMEM((deep, tok, width), BF),
            pltpu.VMEM((deep, tok, width), BF),
            pltpu.VMEM((deep, tok, first.size), BF),
            pltpu.VMEM((deep, tok, second.size), BF),
            pltpu.VMEM((deep, tok, width), BF),
            pltpu.SemaphoreType.DMA((copies,)),
            pltpu.SemaphoreType.DMA((copies,)),
        ],
        compiler_params=pltpu.CompilerParams(
            collective_id=ids.setdefault(("scatter", span), len(ids)),
            has_side_effects=True,
            vmem_limit_bytes=40 << 20,
        ),
        name="scatter_sum",
    )(rows.reshape(n, tok, width))


def forward_stage(layer_in, gate_col, gain_row, gate_mat, up_mat, down_mat, span, ids):
    wide = layer_in.astype(F32)
    normed = (wide * inverse_rms(wide) * gain_row).astype(BF)
    rows = gather_rows(normed, span, ids)
    gate_pre = jnp.dot(rows, gate_mat, preferred_element_type=F32)
    up_val = jnp.dot(rows, up_mat, preferred_element_type=F32)
    activated = (jax.nn.silu(gate_pre) * up_val).astype(BF)
    out = jnp.dot(activated, down_mat, preferred_element_type=F32)
    mixed = scatter_sum((out * gate_col[:, None]).astype(BF), span, ids)
    return (wide + mixed).astype(BF), gate_pre, up_val


def backward_stage(d_in, layer_in, gate_col, gain_row, gate_pre, up_val, gate_mat, up_mat, down_mat, span, ids):
    rows = gather_rows(d_in, span, ids)
    d_out = (gate_col[:, None] * rows.astype(F32)).astype(BF)
    d_act = lax.dot_general(d_out, down_mat, CONTRACT, preferred_element_type=F32)
    sig = jax.nn.sigmoid(gate_pre)
    d_gate = (d_act * up_val * sig * (1.0 + gate_pre * (1.0 - sig))).astype(BF)
    d_up = (d_act * gate_pre * sig).astype(BF)
    summed = lax.dot_general(d_gate, gate_mat, CONTRACT, preferred_element_type=F32)
    summed = summed + lax.dot_general(d_up, up_mat, CONTRACT, preferred_element_type=F32)
    d_norm = scatter_sum(summed.astype(BF), span, ids)
    wide = layer_in.astype(F32)
    inv = inverse_rms(wide)
    scaled = gain_row * d_norm
    inner = jnp.mean(wide * scaled, axis=1, keepdims=True)
    return (d_in.astype(F32) + inv * scaled - wide * (inv * inv * inv) * inner).astype(BF)


def local(inputs, cotangent, norm_gain, routes, route_gates, w_gate, w_up, w_down):
    seg = lax.axis_index("segment")
    segs = lax.axis_size("segment")
    n = lax.axis_size("expert")
    micro, tok, _ = inputs.shape
    mats = (w_gate[0, 0], w_up[0, 0], w_down[0, 0])
    gain_row = norm_gain[0]
    ids = jnp.arange(n, dtype=jnp.int32)
    hit = routes[0][..., None] == ids
    dense = jnp.sum(jnp.where(hit, route_gates[0][..., None], 0.0), axis=2)
    cols = lax.all_to_all(dense.transpose(2, 0, 1), "expert", split_axis=0, concat_axis=0, tiled=True)
    cols = cols.transpose(1, 0, 2).reshape(micro, n * tok)
    ticks = micro + segs - 1
    ids = {}
    ins, outs, pres, ups = [], [], [], []
    incoming = jnp.zeros(inputs.shape[1:], BF)
    for t in range(ticks):
        at = jnp.clip(t - seg, 0, micro - 1)
        span = (max(0, t - micro + 1), min(segs - 1, t))
        layer_in = jnp.where(seg == 0, pick(inputs, at), incoming)
        out, pre, up = forward_stage(layer_in, pick(cols, at), gain_row, *mats, span, ids)
        ins.append(layer_in)
        outs.append(out)
        pres.append(pre)
        ups.append(up)
        if t + 1 < ticks:
            incoming = passed_along(out, 1)
    states = lax.dynamic_slice_in_dim(jnp.stack(outs), seg, micro, 0)
    ins, pres, ups = jnp.stack(ins), jnp.stack(pres), jnp.stack(ups)
    grads = []
    incoming = jnp.zeros(inputs.shape[1:], BF)
    for t in range(ticks):
        at = jnp.clip(t - (segs - 1 - seg), 0, micro - 1)
        span = (max(0, segs - 1 - t), min(segs - 1, segs - 1 - t + micro - 1))
        d_in = jnp.where(seg == segs - 1, pick(cotangent, at), incoming)
        d_prev = backward_stage(
            d_in, pick(ins, at + seg), pick(cols, at), gain_row, pick(pres, at + seg), pick(ups, at + seg), *mats, span, ids
        )
        grads.append(d_prev)
        if t + 1 < ticks:
            incoming = passed_along(d_prev, -1)
    grads = lax.dynamic_slice_in_dim(jnp.stack(grads), segs - 1 - seg, micro, 0)
    return states[None], grads[None]


def solution(mesh):
    placed = (
        P(None, "expert", None),
        P(None, "expert", None),
        P("segment", None),
        P("segment", None, "expert", None),
        P("segment", None, "expert", None),
        P("segment", "expert", None, None),
        P("segment", "expert", None, None),
        P("segment", "expert", None, None),
    )
    return jax.shard_map(
        local,
        mesh=mesh,
        in_specs=placed,
        out_specs=(P("segment", None, "expert", None), P("segment", None, "expert", None)),
        check_vma=False,
    )
```

```python
import jax
import jax.numpy as jnp
from jax import lax
from jax.experimental import pallas as pl
from jax.experimental.pallas import tpu as pltpu
from jax.sharding import PartitionSpec as P

EPS = 1e-06
F32 = jnp.float32
BF = jnp.bfloat16
CONTRACT = (((1,), (1,)), ((), ()))


def passed_along(shard, by):
    peers = lax.axis_size("segment")
    pairs = [(i, i + by) for i in range(peers) if 0 <= i + by < peers]
    return lax.ppermute(shard, "segment", pairs)


def inverse_rms(wide):
    return lax.rsqrt(jnp.mean(wide * wide, axis=1, keepdims=True) + EPS)


def pick(items, index):
    return lax.dynamic_index_in_dim(items, index, 0, keepdims=False)


def place():
    n = lax.axis_size("expert")
    me = lax.axis_index("expert")
    deep = n // 4
    high = me // 4
    low = me % 4
    flip_x = low + 1 - 2 * (low % 2)
    flip_y = (low + 2) % 4
    flip_xy = (flip_x + 2) % 4

    def at(step, corner):
        return lax.rem(high + step, deep) * 4 + corner

    return deep, at, low, flip_x, flip_y, flip_xy


def remote(src, dst, sems, at, target):
    return pltpu.make_async_remote_copy(
        src_ref=src,
        dst_ref=dst,
        send_sem=sems[0].at[at],
        recv_sem=sems[1].at[at],
        device_id={"expert": target},
        device_id_type=pl.DeviceIdType.MESH,
    )


def greet():
    deep, at, low, flip_x, flip_y, _ = place()
    barrier = pltpu.get_barrier_semaphore()
    peers = [at(0, flip_x), at(0, flip_y)] + [at(d, low) for d in range(1, deep)]
    for peer in peers:
        pl.semaphore_signal(barrier, inc=1, device_id={"expert": peer}, device_id_type=pl.DeviceIdType.MESH)
    pl.semaphore_wait(barrier, len(peers))


def halves(width):
    cut = width // 256 * 128
    return pl.ds(0, cut), pl.ds(cut, width - cut)


def gather_body(own, sel, out, column, picked, relay_a, relay_b, *sems):
    deep, at, low, flip_x, flip_y, flip_xy = place()
    cap = out.shape[1]
    first, second = halves(own.shape[1])
    greet()
    to_x, to_y = at(0, flip_x), at(0, flip_y)
    started = []

    def send(src, dst, number, target):
        copy = remote(src, dst, sems, number, target)
        copy.start()
        started.append(copy)
        return copy

    high = at(0, 0) // 4
    along = [None] + [send(own, column.at[high], d, at(d, low)) for d in range(1, deep)]
    plane = []
    for step in range(deep):
        behind = at(deep - step, low)
        level = behind // 4
        if step:
            along[step].wait_recv()
        block = own[...] if step == 0 else column[level]
        picked[step] = jnp.dot(sel[level], block, preferred_element_type=F32).astype(BF)
        base = deep + 6 * step
        diag = picked.at[step, pl.ds(3 * cap, cap)]
        plane.append((
            send(diag.at[:, first], relay_a.at[step], base, to_x),
            send(diag.at[:, second], relay_b.at[step], base + 1, to_y),
            send(picked.at[step, pl.ds(cap, cap)], out.at[behind], base + 2, to_x),
            send(picked.at[step, pl.ds(2 * cap, cap)], out.at[behind], base + 3, to_y),
        ))
        out[behind] = picked[step, 0:cap]
    last = []
    for step in range(deep):
        base = deep + 6 * step
        from_x, from_y = at(deep - step, flip_x), at(deep - step, flip_y)
        plane[step][0].wait_recv()
        last.append(send(relay_a.at[step], out.at[from_x, :, first], base + 4, to_y))
        plane[step][1].wait_recv()
        last.append(send(relay_b.at[step], out.at[from_y, :, second], base + 5, to_x))
    for copies in plane:
        copies[2].wait_recv()
        copies[3].wait_recv()
    for copy in last:
        copy.wait_recv()
    for copy in started:
        copy.wait_send()


def scatter_body(parts, comb, out, slots, relay_a, relay_b, sum_z, in_z, *sems):
    deep, at, low, flip_x, flip_y, flip_xy = place()
    cap = parts.shape[1]
    first, second = halves(out.shape[1])
    greet()
    to_x, to_y = at(0, flip_x), at(0, flip_y)
    started = []

    def send(src, dst, number, target):
        copy = remote(src, dst, sems, number, target)
        copy.start()
        started.append(copy)
        return copy

    order = list(range(1, deep)) + [0]
    early, late = {}, {}
    for step in order:
        base = deep + 6 * step
        diag = at(step, flip_xy)
        early[step] = (
            send(parts.at[diag, :, first], relay_a.at[step], base, to_y),
            send(parts.at[diag, :, second], relay_b.at[step], base + 1, to_x),
            send(parts.at[at(step, flip_x)], slots.at[step, pl.ds(cap, cap)], base + 2, to_x),
            send(parts.at[at(step, flip_y)], slots.at[step, pl.ds(2 * cap, cap)], base + 3, to_y),
        )
        slots[step, 0:cap] = parts[at(step, low)]
    for step in order:
        base = deep + 6 * step
        diag = slots.at[step, pl.ds(3 * cap, cap)]
        early[step][0].wait_recv()
        ex = send(relay_a.at[step], diag.at[:, first], base + 4, to_x)
        early[step][1].wait_recv()
        ey = send(relay_b.at[step], diag.at[:, second], base + 5, to_y)
        late[step] = (ex, ey)

    def joined(step):
        for copy in early[step][2:] + late[step]:
            copy.wait_recv()
        return jnp.dot(comb[at(step, 0) // 4], slots[step], preferred_element_type=F32)

    along = []
    for step in order[:-1]:
        sum_z[step] = joined(step).astype(BF)
        along.append(send(sum_z.at[step], in_z.at[step], step, at(step, low)))
    out[...] = joined(0)
    for step, copy in zip(order, along):
        copy.wait_recv()
        out[...] += in_z[step].astype(F32)
    for copy in started:
        copy.wait_send()


def only_in(span, body):
    def kernel(*refs):
        seg = lax.axis_index("segment")

        @pl.when((seg >= span[0]) & (seg <= span[1]))
        def _():
            body(*refs)

    return kernel


def called(body, kind, span, ids, shape, scratch, copies):
    sems = [pltpu.SemaphoreType.DMA((copies,)), pltpu.SemaphoreType.DMA((copies,))]
    return pl.pallas_call(
        only_in(span, body),
        out_shape=shape,
        in_specs=[pl.BlockSpec(memory_space=pltpu.VMEM)] * 2,
        out_specs=pl.BlockSpec(memory_space=pltpu.VMEM),
        scratch_shapes=scratch + sems,
        compiler_params=pltpu.CompilerParams(
            collective_id=ids.setdefault((kind, span), len(ids)),
            has_side_effects=True,
            vmem_limit_bytes=40 << 20,
        ),
        name=kind,
    )


def gather_rows(rows, sel, span, ids):
    n = lax.axis_size("expert")
    deep = n // 4
    tok, width = rows.shape
    cap = sel.shape[1] // 4
    first, second = halves(width)
    scratch = [
        pltpu.VMEM((deep, tok, width), BF),
        pltpu.VMEM((deep, 4 * cap, width), BF),
        pltpu.VMEM((deep, cap, first.size), BF),
        pltpu.VMEM((deep, cap, second.size), BF),
    ]
    shape = jax.ShapeDtypeStruct((n, cap, width), BF)
    out = called(gather_body, "gather_rows", span, ids, shape, scratch, deep * 7)(rows, sel)
    return out.reshape(n * cap, width)


def scatter_sum(rows, sel, span, ids):
    n = lax.axis_size("expert")
    deep = n // 4
    width = rows.shape[1]
    cap = rows.shape[0] // n
    tok = sel.shape[2]
    first, second = halves(width)
    scratch = [
        pltpu.VMEM((deep, 4 * cap, width), BF),
        pltpu.VMEM((deep, cap, first.size), BF),
        pltpu.VMEM((deep, cap, second.size), BF),
        pltpu.VMEM((deep, tok, width), BF),
        pltpu.VMEM((deep, tok, width), BF),
    ]
    shape = jax.ShapeDtypeStruct((tok, width), F32)
    comb = sel.transpose(0, 2, 1)
    return called(scatter_body, "scatter_sum", span, ids, shape, scratch, deep * 7)(rows.reshape(n, cap, width), comb)


def forward_stage(layer_in, sel, gate_col, gain_row, gate_mat, up_mat, down_mat, span, ids):
    wide = layer_in.astype(F32)
    normed = (wide * inverse_rms(wide) * gain_row).astype(BF)
    rows = gather_rows(normed, sel, span, ids)
    gate_pre = jnp.dot(rows, gate_mat, preferred_element_type=F32)
    up_val = jnp.dot(rows, up_mat, preferred_element_type=F32)
    activated = (jax.nn.silu(gate_pre) * up_val).astype(BF)
    out = jnp.dot(activated, down_mat, preferred_element_type=F32)
    mixed = scatter_sum((out * gate_col[:, None]).astype(BF), sel, span, ids)
    return (wide + mixed).astype(BF), gate_pre, up_val


def backward_stage(d_in, layer_in, sel, gate_col, gain_row, gate_pre, up_val, gate_mat, up_mat, down_mat, span, ids):
    rows = gather_rows(d_in, sel, span, ids)
    d_out = (gate_col[:, None] * rows.astype(F32)).astype(BF)
    d_act = lax.dot_general(d_out, down_mat, CONTRACT, preferred_element_type=F32)
    sig = jax.nn.sigmoid(gate_pre)
    d_gate = (d_act * up_val * sig * (1.0 + gate_pre * (1.0 - sig))).astype(BF)
    d_up = (d_act * gate_pre * sig).astype(BF)
    summed = lax.dot_general(d_gate, gate_mat, CONTRACT, preferred_element_type=F32)
    summed = summed + lax.dot_general(d_up, up_mat, CONTRACT, preferred_element_type=F32)
    d_norm = scatter_sum(summed.astype(BF), sel, span, ids)
    wide = layer_in.astype(F32)
    inv = inverse_rms(wide)
    scaled = gain_row * d_norm
    inner = jnp.mean(wide * scaled, axis=1, keepdims=True)
    return (d_in.astype(F32) + inv * scaled - wide * (inv * inv * inv) * inner).astype(BF)


def local(inputs, cotangent, norm_gain, routes, route_gates, w_gate, w_up, w_down):
    seg = lax.axis_index("segment")
    segs = lax.axis_size("segment")
    n = lax.axis_size("expert")
    micro, tok, _ = inputs.shape
    mats = (w_gate[0, 0], w_up[0, 0], w_down[0, 0])
    gain_row = norm_gain[0]
    cap = min(tok, 4 * tok * routes.shape[3] // (3 * n))
    deep = n // 4
    hit = routes[0][..., None] == jnp.arange(n, dtype=jnp.int32)
    dense = jnp.sum(jnp.where(hit, route_gates[0][..., None], 0.0), axis=2)
    named = jnp.any(hit, axis=2)
    counted = named.astype(jnp.int32)
    before = jnp.cumsum(counted, axis=1) - counted
    spot = jnp.where(named, before, -1).transpose(2, 0, 1)[:, :, None, :]
    taken = spot == jnp.arange(cap, dtype=jnp.int32)[:, None]
    cols = jnp.sum(jnp.where(taken, dense.transpose(2, 0, 1)[:, :, None, :], 0.0), axis=3)
    cols = lax.all_to_all(cols, "expert", split_axis=0, concat_axis=0, tiled=True)
    cols = cols.transpose(1, 0, 2).reshape(micro, n * cap)
    low = lax.axis_index("expert") % 4
    corners = jnp.bitwise_xor(low, jnp.arange(4, dtype=jnp.int32))
    sels = jnp.take(taken.astype(BF).reshape(deep, 4, micro, cap, tok), corners, axis=1)
    sels = sels.transpose(0, 2, 1, 3, 4).reshape(deep, micro, 4 * cap, tok)
    columns = [[level * 4 + corner for level in range(deep)] for corner in range(4)]
    sels = lax.all_to_all(sels, "expert", split_axis=0, concat_axis=0, tiled=True, axis_index_groups=columns)
    sels = sels.transpose(1, 0, 2, 3)
    ticks = micro + segs - 1
    ids = {}
    ins, outs, pres, ups = [], [], [], []
    incoming = jnp.zeros(inputs.shape[1:], BF)
    for t in range(ticks):
        at = jnp.clip(t - seg, 0, micro - 1)
        span = (max(0, t - micro + 1), min(segs - 1, t))
        layer_in = jnp.where(seg == 0, pick(inputs, at), incoming)
        out, pre, up = forward_stage(layer_in, pick(sels, at), pick(cols, at), gain_row, *mats, span, ids)
        ins.append(layer_in)
        outs.append(out)
        pres.append(pre)
        ups.append(up)
        if t + 1 < ticks:
            incoming = passed_along(out, 1)
    states = lax.dynamic_slice_in_dim(jnp.stack(outs), seg, micro, 0)
    ins, pres, ups = jnp.stack(ins), jnp.stack(pres), jnp.stack(ups)
    grads = []
    incoming = jnp.zeros(inputs.shape[1:], BF)
    for t in range(ticks):
        at = jnp.clip(t - (segs - 1 - seg), 0, micro - 1)
        span = (max(0, segs - 1 - t), min(segs - 1, segs - 1 - t + micro - 1))
        d_in = jnp.where(seg == segs - 1, pick(cotangent, at), incoming)
        d_prev = backward_stage(
            d_in, pick(ins, at + seg), pick(sels, at), pick(cols, at), gain_row, pick(pres, at + seg), pick(ups, at + seg), *mats, span, ids
        )
        grads.append(d_prev)
        if t + 1 < ticks:
            incoming = passed_along(d_prev, -1)
    grads = lax.dynamic_slice_in_dim(jnp.stack(grads), segs - 1 - seg, micro, 0)
    return states[None], grads[None]


def solution(mesh):
    placed = (
        P(None, "expert", None),
        P(None, "expert", None),
        P("segment", None),
        P("segment", None, "expert", None),
        P("segment", None, "expert", None),
        P("segment", "expert", None, None),
        P("segment", "expert", None, None),
        P("segment", "expert", None, None),
    )
    return jax.shard_map(
        local,
        mesh=mesh,
        in_specs=placed,
        out_specs=(P("segment", None, "expert", None), P("segment", None, "expert", None)),
        check_vma=False,
    )
```

```python
import jax
import jax.numpy as jnp
from jax import lax
from jax.experimental import pallas as pl
from jax.experimental.pallas import tpu as pltpu
from jax.sharding import PartitionSpec as P

EPS = 1e-06
F32 = jnp.float32
BF = jnp.bfloat16
CONTRACT = (((1,), (1,)), ((), ()))


def passed_along(shard, by):
    peers = lax.axis_size("segment")
    pairs = [(i, i + by) for i in range(peers) if 0 <= i + by < peers]
    return lax.ppermute(shard, "segment", pairs)


def inverse_rms(wide):
    return lax.rsqrt(jnp.mean(wide * wide, axis=1, keepdims=True) + EPS)


def pick(items, index):
    return lax.dynamic_index_in_dim(items, index, 0, keepdims=False)


def place():
    n = lax.axis_size("expert")
    me = lax.axis_index("expert")
    deep = n // 4
    high = me // 4
    low = me % 4
    flip_x = low + 1 - 2 * (low % 2)
    flip_y = (low + 2) % 4
    flip_xy = (flip_x + 2) % 4

    def at(step, corner):
        return lax.rem(high + step, deep) * 4 + corner

    return deep, at, low, flip_x, flip_y, flip_xy


def remote(src, dst, sems, at, target):
    return pltpu.make_async_remote_copy(
        src_ref=src,
        dst_ref=dst,
        send_sem=sems[0].at[at],
        recv_sem=sems[1].at[at],
        device_id={"expert": target},
        device_id_type=pl.DeviceIdType.MESH,
    )


def greet():
    deep, at, low, flip_x, flip_y, _ = place()
    barrier = pltpu.get_barrier_semaphore()
    peers = [at(0, flip_x), at(0, flip_y)] + [at(d, low) for d in range(1, deep)]
    for peer in peers:
        pl.semaphore_signal(barrier, inc=1, device_id={"expert": peer}, device_id_type=pl.DeviceIdType.MESH)
    pl.semaphore_wait(barrier, len(peers))


def halves(width):
    cut = width // 256 * 128
    return pl.ds(0, cut), pl.ds(cut, width - cut)


def gather_body(own, sel, out, column, picked, relay_a, relay_b, *sems):
    deep, at, low, flip_x, flip_y, flip_xy = place()
    cap = out.shape[1]
    first, second = halves(own.shape[1])
    greet()
    to_x, to_y = at(0, flip_x), at(0, flip_y)
    started = []

    def send(src, dst, number, target):
        copy = remote(src, dst, sems, number, target)
        copy.start()
        started.append(copy)
        return copy

    cuts = (first, second)
    high = at(0, 0) // 4
    along, plane, last = {}, {}, []
    for half, cols in enumerate(cuts):
        for d in range(1, deep):
            along[d, half] = send(own.at[:, cols], column.at[high, :, cols], 2 * d + half, at(d, low))

    def choose(step, half):
        cols = cuts[half]
        behind = at(deep - step, low)
        level = behind // 4
        if step:
            along[step, half].wait_recv()
        block = own[:, cols] if step == 0 else column[level, :, cols]
        picked[step, :, cols] = jnp.dot(sel[level], block, preferred_element_type=F32).astype(BF)
        base = 2 * deep + 8 * step + 4 * half
        diag = picked.at[step, pl.ds(3 * cap, cap), cols]
        dst = out.at[behind, :, cols]
        plane[step, half] = (
            send(diag, (relay_a, relay_b)[half].at[step], base, (to_x, to_y)[half]),
            send(picked.at[step, pl.ds(cap, cap), cols], dst, base + 1, to_x),
            send(picked.at[step, pl.ds(2 * cap, cap), cols], dst, base + 2, to_y),
        )
        out[behind, :, cols] = picked[step, 0:cap, cols]

    def relay(step, half):
        base = 2 * deep + 8 * step + 4 * half
        origin = at(deep - step, (flip_x, flip_y)[half])
        plane[step, half][0].wait_recv()
        dst = out.at[origin, :, cuts[half]]
        last.append(send((relay_a, relay_b)[half].at[step], dst, base + 3, (to_y, to_x)[half]))

    items = [(0, 0), (0, 1)] + [(step, half) for half in range(2) for step in range(1, deep)]
    for number, item in enumerate(items):
        choose(*item)
        if number:
            relay(*items[number - 1])
    relay(*items[-1])
    for copies in plane.values():
        copies[1].wait_recv()
        copies[2].wait_recv()
    for copy in last:
        copy.wait_recv()
    for copy in started:
        copy.wait_send()


def scatter_body(parts, comb, out, slots, relay_a, relay_b, sum_z, in_z, *sems):
    deep, at, low, flip_x, flip_y, flip_xy = place()
    cap = parts.shape[1]
    first, second = halves(out.shape[1])
    greet()
    to_x, to_y = at(0, flip_x), at(0, flip_y)
    started = []

    def send(src, dst, number, target):
        copy = remote(src, dst, sems, number, target)
        copy.start()
        started.append(copy)
        return copy

    cuts = (first, second)
    items = [(step, half) for half in range(2) for step in range(1, deep)] + [(0, 0), (0, 1)]
    early, late, along = {}, {}, {}
    for step, half in items:
        cols = cuts[half]
        base = 2 * deep + 8 * step + 4 * half
        diag = parts.at[at(step, flip_xy), :, cols]
        early[step, half] = (
            send(diag, (relay_a, relay_b)[half].at[step], base, (to_y, to_x)[half]),
            send(parts.at[at(step, flip_x), :, cols], slots.at[step, pl.ds(cap, cap), cols], base + 1, to_x),
            send(parts.at[at(step, flip_y), :, cols], slots.at[step, pl.ds(2 * cap, cap), cols], base + 2, to_y),
        )
    for step in range(deep):
        slots[step, 0:cap] = parts[at(step, low)]

    def relay(step, half):
        base = 2 * deep + 8 * step + 4 * half
        early[step, half][0].wait_recv()
        dst = slots.at[step, pl.ds(3 * cap, cap), cuts[half]]
        late[step, half] = send((relay_a, relay_b)[half].at[step], dst, base + 3, (to_x, to_y)[half])

    def join(step, half):
        cols = cuts[half]
        for copy in early[step, half][1:] + (late[step, half],):
            copy.wait_recv()
        joined = jnp.dot(comb[at(step, 0) // 4], slots[step, :, cols], preferred_element_type=F32)
        if step == 0:
            out[:, cols] = joined
            return
        sum_z[step, :, cols] = joined.astype(BF)
        dst = in_z.at[step, :, cols]
        along[step, half] = send(sum_z.at[step, :, cols], dst, 2 * step + half, at(step, low))

    for number, item in enumerate(items):
        relay(*item)
        if number > 1:
            join(*items[number - 2])
    for item in items[-2:]:
        join(*item)
    for (step, half), copy in along.items():
        copy.wait_recv()
        out[:, cuts[half]] += in_z[step, :, cuts[half]].astype(F32)
    for copy in started:
        copy.wait_send()


def only_in(span, body):
    def kernel(*refs):
        seg = lax.axis_index("segment")

        @pl.when((seg >= span[0]) & (seg <= span[1]))
        def _():
            body(*refs)

    return kernel


def called(body, kind, span, ids, shape, scratch, copies):
    sems = [pltpu.SemaphoreType.DMA((copies,)), pltpu.SemaphoreType.DMA((copies,))]
    return pl.pallas_call(
        only_in(span, body),
        out_shape=shape,
        in_specs=[pl.BlockSpec(memory_space=pltpu.VMEM)] * 2,
        out_specs=pl.BlockSpec(memory_space=pltpu.VMEM),
        scratch_shapes=scratch + sems,
        compiler_params=pltpu.CompilerParams(
            collective_id=ids.setdefault((kind, span), len(ids)),
            has_side_effects=True,
            vmem_limit_bytes=40 << 20,
        ),
        name=kind,
    )


def gather_rows(rows, sel, span, ids):
    n = lax.axis_size("expert")
    deep = n // 4
    tok, width = rows.shape
    cap = sel.shape[1] // 4
    first, second = halves(width)
    scratch = [
        pltpu.VMEM((deep, tok, width), BF),
        pltpu.VMEM((deep, 4 * cap, width), BF),
        pltpu.VMEM((deep, cap, first.size), BF),
        pltpu.VMEM((deep, cap, second.size), BF),
    ]
    shape = jax.ShapeDtypeStruct((n, cap, width), BF)
    out = called(gather_body, "gather_rows", span, ids, shape, scratch, deep * 10)(rows, sel)
    return out.reshape(n * cap, width)


def scatter_sum(rows, sel, span, ids):
    n = lax.axis_size("expert")
    deep = n // 4
    width = rows.shape[1]
    cap = rows.shape[0] // n
    tok = sel.shape[2]
    first, second = halves(width)
    scratch = [
        pltpu.VMEM((deep, 4 * cap, width), BF),
        pltpu.VMEM((deep, cap, first.size), BF),
        pltpu.VMEM((deep, cap, second.size), BF),
        pltpu.VMEM((deep, tok, width), BF),
        pltpu.VMEM((deep, tok, width), BF),
    ]
    shape = jax.ShapeDtypeStruct((tok, width), F32)
    comb = sel.transpose(0, 2, 1)
    return called(scatter_body, "scatter_sum", span, ids, shape, scratch, deep * 10)(rows.reshape(n, cap, width), comb)


def forward_stage(layer_in, sel, gate_col, gain_row, gate_mat, up_mat, down_mat, span, ids):
    wide = layer_in.astype(F32)
    normed = (wide * inverse_rms(wide) * gain_row).astype(BF)
    rows = gather_rows(normed, sel, span, ids)
    gate_pre = jnp.dot(rows, gate_mat, preferred_element_type=F32)
    up_val = jnp.dot(rows, up_mat, preferred_element_type=F32)
    activated = (jax.nn.silu(gate_pre) * up_val).astype(BF)
    out = jnp.dot(activated, down_mat, preferred_element_type=F32)
    mixed = scatter_sum((out * gate_col[:, None]).astype(BF), sel, span, ids)
    return (wide + mixed).astype(BF), gate_pre, up_val


def backward_stage(d_in, layer_in, sel, gate_col, gain_row, gate_pre, up_val, gate_mat, up_mat, down_mat, span, ids):
    rows = gather_rows(d_in, sel, span, ids)
    d_out = (gate_col[:, None] * rows.astype(F32)).astype(BF)
    d_act = lax.dot_general(d_out, down_mat, CONTRACT, preferred_element_type=F32)
    sig = jax.nn.sigmoid(gate_pre)
    d_gate = (d_act * up_val * sig * (1.0 + gate_pre * (1.0 - sig))).astype(BF)
    d_up = (d_act * gate_pre * sig).astype(BF)
    summed = lax.dot_general(d_gate, gate_mat, CONTRACT, preferred_element_type=F32)
    summed = summed + lax.dot_general(d_up, up_mat, CONTRACT, preferred_element_type=F32)
    d_norm = scatter_sum(summed.astype(BF), sel, span, ids)
    wide = layer_in.astype(F32)
    inv = inverse_rms(wide)
    scaled = gain_row * d_norm
    inner = jnp.mean(wide * scaled, axis=1, keepdims=True)
    return (d_in.astype(F32) + inv * scaled - wide * (inv * inv * inv) * inner).astype(BF)


def local(inputs, cotangent, norm_gain, routes, route_gates, w_gate, w_up, w_down):
    seg = lax.axis_index("segment")
    segs = lax.axis_size("segment")
    n = lax.axis_size("expert")
    micro, tok, _ = inputs.shape
    mats = (w_gate[0, 0], w_up[0, 0], w_down[0, 0])
    gain_row = norm_gain[0]
    cap = min(tok, 4 * tok * routes.shape[3] // (3 * n))
    deep = n // 4
    hit = routes[0][..., None] == jnp.arange(n, dtype=jnp.int32)
    dense = jnp.sum(jnp.where(hit, route_gates[0][..., None], 0.0), axis=2)
    named = jnp.any(hit, axis=2)
    counted = named.astype(jnp.int32)
    before = jnp.cumsum(counted, axis=1) - counted
    spot = jnp.where(named, before, -1).transpose(2, 0, 1)[:, :, None, :]
    taken = spot == jnp.arange(cap, dtype=jnp.int32)[:, None]
    cols = jnp.sum(jnp.where(taken, dense.transpose(2, 0, 1)[:, :, None, :], 0.0), axis=3)
    cols = lax.all_to_all(cols, "expert", split_axis=0, concat_axis=0, tiled=True)
    cols = cols.transpose(1, 0, 2).reshape(micro, n * cap)
    low = lax.axis_index("expert") % 4
    corners = jnp.bitwise_xor(low, jnp.arange(4, dtype=jnp.int32))
    sels = jnp.take(taken.astype(BF).reshape(deep, 4, micro, cap, tok), corners, axis=1)
    sels = sels.transpose(0, 2, 1, 3, 4).reshape(deep, micro, 4 * cap, tok)
    columns = [[level * 4 + corner for level in range(deep)] for corner in range(4)]
    sels = lax.all_to_all(sels, "expert", split_axis=0, concat_axis=0, tiled=True, axis_index_groups=columns)
    sels = sels.transpose(1, 0, 2, 3)
    ticks = micro + segs - 1
    ids = {}
    ins, outs, pres, ups = [], [], [], []
    incoming = jnp.zeros(inputs.shape[1:], BF)
    for t in range(ticks):
        at = jnp.clip(t - seg, 0, micro - 1)
        span = (max(0, t - micro + 1), min(segs - 1, t))
        layer_in = jnp.where(seg == 0, pick(inputs, at), incoming)
        out, pre, up = forward_stage(layer_in, pick(sels, at), pick(cols, at), gain_row, *mats, span, ids)
        ins.append(layer_in)
        outs.append(out)
        pres.append(pre)
        ups.append(up)
        if t + 1 < ticks:
            incoming = passed_along(out, 1)
    states = lax.dynamic_slice_in_dim(jnp.stack(outs), seg, micro, 0)
    ins, pres, ups = jnp.stack(ins), jnp.stack(pres), jnp.stack(ups)
    grads = []
    incoming = jnp.zeros(inputs.shape[1:], BF)
    for t in range(ticks):
        at = jnp.clip(t - (segs - 1 - seg), 0, micro - 1)
        span = (max(0, segs - 1 - t), min(segs - 1, segs - 1 - t + micro - 1))
        d_in = jnp.where(seg == segs - 1, pick(cotangent, at), incoming)
        d_prev = backward_stage(
            d_in, pick(ins, at + seg), pick(sels, at), pick(cols, at), gain_row, pick(pres, at + seg), pick(ups, at + seg), *mats, span, ids
        )
        grads.append(d_prev)
        if t + 1 < ticks:
            incoming = passed_along(d_prev, -1)
    grads = lax.dynamic_slice_in_dim(jnp.stack(grads), segs - 1 - seg, micro, 0)
    return states[None], grads[None]


def solution(mesh):
    placed = (
        P(None, "expert", None),
        P(None, "expert", None),
        P("segment", None),
        P("segment", None, "expert", None),
        P("segment", None, "expert", None),
        P("segment", "expert", None, None),
        P("segment", "expert", None, None),
        P("segment", "expert", None, None),
    )
    return jax.shard_map(
        local,
        mesh=mesh,
        in_specs=placed,
        out_specs=(P("segment", None, "expert", None), P("segment", None, "expert", None)),
        check_vma=False,
    )
```

```python
import jax
import jax.numpy as jnp
from jax import lax
from jax.experimental import pallas as pl
from jax.experimental.pallas import tpu as pltpu
from jax.sharding import PartitionSpec as P

EPS = 1e-06
F32 = jnp.float32
BF = jnp.bfloat16
CONTRACT = (((1,), (1,)), ((), ()))


def passed_along(shard, by):
    peers = lax.axis_size("segment")
    pairs = [(i, i + by) for i in range(peers) if 0 <= i + by < peers]
    return lax.ppermute(shard, "segment", pairs)


def inverse_rms(wide):
    return lax.rsqrt(jnp.mean(wide * wide, axis=1, keepdims=True) + EPS)


def pick(items, index):
    return lax.dynamic_index_in_dim(items, index, 0, keepdims=False)


def place():
    n = lax.axis_size("expert")
    me = lax.axis_index("expert")
    deep = n // 4
    high = me // 4
    low = me % 4
    flip_x = low + 1 - 2 * (low % 2)
    flip_y = (low + 2) % 4
    flip_xy = (flip_x + 2) % 4

    def at(step, corner):
        return lax.rem(high + step, deep) * 4 + corner

    return deep, at, low, flip_x, flip_y, flip_xy


def remote(src, dst, sems, at, target):
    return pltpu.make_async_remote_copy(
        src_ref=src,
        dst_ref=dst,
        send_sem=sems[0].at[at],
        recv_sem=sems[1].at[at],
        device_id={"expert": target},
        device_id_type=pl.DeviceIdType.MESH,
    )


def greet():
    deep, at, low, flip_x, flip_y, _ = place()
    barrier = pltpu.get_barrier_semaphore()
    peers = [at(0, flip_x), at(0, flip_y)] + [at(d, low) for d in range(1, deep)]
    for peer in peers:
        pl.semaphore_signal(barrier, inc=1, device_id={"expert": peer}, device_id_type=pl.DeviceIdType.MESH)
    pl.semaphore_wait(barrier, len(peers))


def halves(width):
    cut = width // 256 * 128
    return pl.ds(0, cut), pl.ds(cut, width - cut)


def gather_body(own, sel, out, column, picked, relay_a, relay_b, *sems):
    deep, at, low, flip_x, flip_y, flip_xy = place()
    cap = out.shape[1]
    first, second = halves(own.shape[1])
    greet()
    to_x, to_y = at(0, flip_x), at(0, flip_y)
    started = []

    def send(src, dst, number, target):
        copy = remote(src, dst, sems, number, target)
        copy.start()
        started.append(copy)
        return copy

    cuts = (first, second)
    high = at(0, 0) // 4
    along, plane, last = {}, {}, []
    for half, cols in enumerate(cuts):
        for d in range(1, deep):
            along[d, half] = send(own.at[:, cols], column.at[high, :, cols], 2 * d + half, at(d, low))

    def choose(step, half):
        cols = cuts[half]
        behind = at(deep - step, low)
        level = behind // 4
        if step:
            along[step, half].wait_recv()
        block = own[:, cols] if step == 0 else column[level, :, cols]
        picked[step, :, cols] = jnp.dot(sel[level], block, preferred_element_type=F32).astype(BF)
        base = 2 * deep + 8 * step + 4 * half
        diag = picked.at[step, pl.ds(3 * cap, cap), cols]
        dst = out.at[behind, :, cols]
        plane[step, half] = (
            send(diag, (relay_a, relay_b)[half].at[step], base, (to_x, to_y)[half]),
            send(picked.at[step, pl.ds(cap, cap), cols], dst, base + 1, to_x),
            send(picked.at[step, pl.ds(2 * cap, cap), cols], dst, base + 2, to_y),
        )
        out[behind, :, cols] = picked[step, 0:cap, cols]

    def relay(step, half):
        base = 2 * deep + 8 * step + 4 * half
        origin = at(deep - step, (flip_x, flip_y)[half])
        plane[step, half][0].wait_recv()
        dst = out.at[origin, :, cuts[half]]
        last.append(send((relay_a, relay_b)[half].at[step], dst, base + 3, (to_y, to_x)[half]))

    items = [(0, 0), (0, 1)] + [(step, half) for half in range(2) for step in range(1, deep)]
    for number, item in enumerate(items):
        choose(*item)
        if number:
            relay(*items[number - 1])
    relay(*items[-1])
    for copies in plane.values():
        copies[1].wait_recv()
        copies[2].wait_recv()
    for copy in last:
        copy.wait_recv()
    for copy in started:
        copy.wait_send()


def scatter_body(parts, comb, out, slots, relay_a, relay_b, sum_z, in_z, *sems):
    deep, at, low, flip_x, flip_y, flip_xy = place()
    cap = parts.shape[1]
    first, second = halves(out.shape[1])
    greet()
    to_x, to_y = at(0, flip_x), at(0, flip_y)
    started = []

    def send(src, dst, number, target):
        copy = remote(src, dst, sems, number, target)
        copy.start()
        started.append(copy)
        return copy

    cuts = (first, second)
    items = [(step, half) for half in range(2) for step in range(1, deep)] + [(0, 0), (0, 1)]
    early, late, along = {}, {}, {}

    def launch(step, half):
        cols = cuts[half]
        base = 2 * deep + 8 * step + 4 * half
        diag = parts.at[at(step, flip_xy), :, cols]
        early[step, half] = (
            send(diag, (relay_a, relay_b)[half].at[step], base, (to_y, to_x)[half]),
            send(parts.at[at(step, flip_x), :, cols], slots.at[step, pl.ds(cap, cap), cols], base + 1, to_x),
            send(parts.at[at(step, flip_y), :, cols], slots.at[step, pl.ds(2 * cap, cap), cols], base + 2, to_y),
        )

    for item in items[:4]:
        launch(*item)
    for step in range(deep):
        slots[step, 0:cap] = parts[at(step, low)]

    def relay(step, half):
        base = 2 * deep + 8 * step + 4 * half
        early[step, half][0].wait_recv()
        dst = slots.at[step, pl.ds(3 * cap, cap), cuts[half]]
        late[step, half] = send((relay_a, relay_b)[half].at[step], dst, base + 3, (to_x, to_y)[half])

    def join(step, half):
        cols = cuts[half]
        for copy in early[step, half][1:] + (late[step, half],):
            copy.wait_recv()
        joined = jnp.dot(comb[at(step, 0) // 4], slots[step, :, cols], preferred_element_type=F32)
        if step == 0:
            out[:, cols] = joined
            return
        sum_z[step, :, cols] = joined.astype(BF)
        dst = in_z.at[step, :, cols]
        along[step, half] = send(sum_z.at[step, :, cols], dst, 2 * step + half, at(step, low))

    for number, item in enumerate(items):
        relay(*item)
        if number + 4 < len(items):
            launch(*items[number + 4])
        if number > 1:
            join(*items[number - 2])
    for item in items[-2:]:
        join(*item)
    for (step, half), copy in along.items():
        copy.wait_recv()
        out[:, cuts[half]] += in_z[step, :, cuts[half]].astype(F32)
    for copy in started:
        copy.wait_send()


def only_in(span, body):
    def kernel(*refs):
        seg = lax.axis_index("segment")

        @pl.when((seg >= span[0]) & (seg <= span[1]))
        def _():
            body(*refs)

    return kernel


def called(body, kind, span, ids, shape, scratch, copies):
    sems = [pltpu.SemaphoreType.DMA((copies,)), pltpu.SemaphoreType.DMA((copies,))]
    return pl.pallas_call(
        only_in(span, body),
        out_shape=shape,
        in_specs=[pl.BlockSpec(memory_space=pltpu.VMEM)] * 2,
        out_specs=pl.BlockSpec(memory_space=pltpu.VMEM),
        scratch_shapes=scratch + sems,
        compiler_params=pltpu.CompilerParams(
            collective_id=ids.setdefault((kind, span), len(ids)),
            has_side_effects=True,
            vmem_limit_bytes=40 << 20,
        ),
        name=kind,
    )


def gather_rows(rows, sel, span, ids):
    n = lax.axis_size("expert")
    deep = n // 4
    tok, width = rows.shape
    cap = sel.shape[1] // 4
    first, second = halves(width)
    scratch = [
        pltpu.VMEM((deep, tok, width), BF),
        pltpu.VMEM((deep, 4 * cap, width), BF),
        pltpu.VMEM((deep, cap, first.size), BF),
        pltpu.VMEM((deep, cap, second.size), BF),
    ]
    shape = jax.ShapeDtypeStruct((n, cap, width), BF)
    out = called(gather_body, "gather_rows", span, ids, shape, scratch, deep * 10)(rows, sel)
    return out.reshape(n * cap, width)


def scatter_sum(rows, sel, span, ids):
    n = lax.axis_size("expert")
    deep = n // 4
    width = rows.shape[1]
    cap = rows.shape[0] // n
    tok = sel.shape[2]
    first, second = halves(width)
    scratch = [
        pltpu.VMEM((deep, 4 * cap, width), BF),
        pltpu.VMEM((deep, cap, first.size), BF),
        pltpu.VMEM((deep, cap, second.size), BF),
        pltpu.VMEM((deep, tok, width), BF),
        pltpu.VMEM((deep, tok, width), BF),
    ]
    shape = jax.ShapeDtypeStruct((tok, width), F32)
    comb = sel.transpose(0, 2, 1)
    return called(scatter_body, "scatter_sum", span, ids, shape, scratch, deep * 10)(rows.reshape(n, cap, width), comb)


def forward_stage(layer_in, sel, gate_col, gain_row, gate_mat, up_mat, down_mat, span, ids):
    wide = layer_in.astype(F32)
    normed = (wide * inverse_rms(wide) * gain_row).astype(BF)
    rows = gather_rows(normed, sel, span, ids)
    gate_pre = jnp.dot(rows, gate_mat, preferred_element_type=F32)
    up_val = jnp.dot(rows, up_mat, preferred_element_type=F32)
    activated = (jax.nn.silu(gate_pre) * up_val).astype(BF)
    out = jnp.dot(activated, down_mat, preferred_element_type=F32)
    mixed = scatter_sum((out * gate_col[:, None]).astype(BF), sel, span, ids)
    return (wide + mixed).astype(BF), gate_pre, up_val


def backward_stage(d_in, layer_in, sel, gate_col, gain_row, gate_pre, up_val, gate_mat, up_mat, down_mat, span, ids):
    rows = gather_rows(d_in, sel, span, ids)
    d_out = (gate_col[:, None] * rows.astype(F32)).astype(BF)
    d_act = lax.dot_general(d_out, down_mat, CONTRACT, preferred_element_type=F32)
    sig = jax.nn.sigmoid(gate_pre)
    d_gate = (d_act * up_val * sig * (1.0 + gate_pre * (1.0 - sig))).astype(BF)
    d_up = (d_act * gate_pre * sig).astype(BF)
    summed = lax.dot_general(d_gate, gate_mat, CONTRACT, preferred_element_type=F32)
    summed = summed + lax.dot_general(d_up, up_mat, CONTRACT, preferred_element_type=F32)
    d_norm = scatter_sum(summed.astype(BF), sel, span, ids)
    wide = layer_in.astype(F32)
    inv = inverse_rms(wide)
    scaled = gain_row * d_norm
    inner = jnp.mean(wide * scaled, axis=1, keepdims=True)
    return (d_in.astype(F32) + inv * scaled - wide * (inv * inv * inv) * inner).astype(BF)


def local(inputs, cotangent, norm_gain, routes, route_gates, w_gate, w_up, w_down):
    seg = lax.axis_index("segment")
    segs = lax.axis_size("segment")
    n = lax.axis_size("expert")
    micro, tok, _ = inputs.shape
    mats = (w_gate[0, 0], w_up[0, 0], w_down[0, 0])
    gain_row = norm_gain[0]
    cap = min(tok, 4 * tok * routes.shape[3] // (3 * n))
    deep = n // 4
    hit = routes[0][..., None] == jnp.arange(n, dtype=jnp.int32)
    dense = jnp.sum(jnp.where(hit, route_gates[0][..., None], 0.0), axis=2)
    named = jnp.any(hit, axis=2)
    counted = named.astype(jnp.int32)
    before = jnp.cumsum(counted, axis=1) - counted
    spot = jnp.where(named, before, -1).transpose(2, 0, 1)[:, :, None, :]
    taken = spot == jnp.arange(cap, dtype=jnp.int32)[:, None]
    cols = jnp.sum(jnp.where(taken, dense.transpose(2, 0, 1)[:, :, None, :], 0.0), axis=3)
    cols = lax.all_to_all(cols, "expert", split_axis=0, concat_axis=0, tiled=True)
    cols = cols.transpose(1, 0, 2).reshape(micro, n * cap)
    low = lax.axis_index("expert") % 4
    corners = jnp.bitwise_xor(low, jnp.arange(4, dtype=jnp.int32))
    sels = jnp.take(taken.astype(BF).reshape(deep, 4, micro, cap, tok), corners, axis=1)
    sels = sels.transpose(0, 2, 1, 3, 4).reshape(deep, micro, 4 * cap, tok)
    columns = [[level * 4 + corner for level in range(deep)] for corner in range(4)]
    sels = lax.all_to_all(sels, "expert", split_axis=0, concat_axis=0, tiled=True, axis_index_groups=columns)
    sels = sels.transpose(1, 0, 2, 3)
    ticks = micro + segs - 1
    ids = {}
    ins, outs, pres, ups = [], [], [], []
    incoming = jnp.zeros(inputs.shape[1:], BF)
    for t in range(ticks):
        at = jnp.clip(t - seg, 0, micro - 1)
        span = (max(0, t - micro + 1), min(segs - 1, t))
        layer_in = jnp.where(seg == 0, pick(inputs, at), incoming)
        out, pre, up = forward_stage(layer_in, pick(sels, at), pick(cols, at), gain_row, *mats, span, ids)
        ins.append(layer_in)
        outs.append(out)
        pres.append(pre)
        ups.append(up)
        if t + 1 < ticks:
            incoming = passed_along(out, 1)
    states = lax.dynamic_slice_in_dim(jnp.stack(outs), seg, micro, 0)
    ins, pres, ups = jnp.stack(ins), jnp.stack(pres), jnp.stack(ups)
    grads = []
    incoming = jnp.zeros(inputs.shape[1:], BF)
    for t in range(ticks):
        at = jnp.clip(t - (segs - 1 - seg), 0, micro - 1)
        span = (max(0, segs - 1 - t), min(segs - 1, segs - 1 - t + micro - 1))
        d_in = jnp.where(seg == segs - 1, pick(cotangent, at), incoming)
        d_prev = backward_stage(
            d_in, pick(ins, at + seg), pick(sels, at), pick(cols, at), gain_row, pick(pres, at + seg), pick(ups, at + seg), *mats, span, ids
        )
        grads.append(d_prev)
        if t + 1 < ticks:
            incoming = passed_along(d_prev, -1)
    grads = lax.dynamic_slice_in_dim(jnp.stack(grads), segs - 1 - seg, micro, 0)
    return states[None], grads[None]


def solution(mesh):
    placed = (
        P(None, "expert", None),
        P(None, "expert", None),
        P("segment", None),
        P("segment", None, "expert", None),
        P("segment", None, "expert", None),
        P("segment", "expert", None, None),
        P("segment", "expert", None, None),
        P("segment", "expert", None, None),
    )
    return jax.shard_map(
        local,
        mesh=mesh,
        in_specs=placed,
        out_specs=(P("segment", None, "expert", None), P("segment", None, "expert", None)),
        check_vma=False,
    )
```
